32 devices in a mesh: dp: 8 (over y, x, core), mp: 4 (over z).
Axes of the slice: x: 2, y: 2, z: 4, core: 2. Of those that a mesh axis runs over, the one named last changes fastest.
Arguments:
- tokens: bfloat16 [4096, 4096], P('dp'), may hold values from -6 to 6
- cache: bfloat16 [192, 128, 896], P('dp'), may hold values from -220 to 220
- nb_row: int32 [64, 2], P('dp'), may hold values from 0 to 23
- nb_owner: int32 [64, 2], P('dp'), may hold values from 0 to 7, all different within a row; in each aligned block of 8 rows (0 to 7, 8 to 15, ...) at most 3 rows name the same one
- nb_len: int32 [64, 2], P('dp'), may hold values from 32 to 128, as said below
- w_query: bfloat16 [4096, 4096], P('dp', 'mp'), may hold values from -0.09375 to 0.09375
- w_key: bfloat16 [896, 4096], P('dp', 'mp'), may hold values from -0.1875 to 0.1875
- w_value: bfloat16 [896, 4096], P('dp', 'mp'), may hold values from -0.1875 to 0.1875
- w_out: bfloat16 [4096, 4096], P('mp', 'dp'), may hold values from -0.09375 to 0.09375
- grad_out: bfloat16 [4096, 4096], P('dp'), may hold values from -6 to 6
Outputs:
- mixed: bfloat16 [4096, 4096], P('dp', 'mp')
- grad_tokens: bfloat16 [4096, 4096], P('dp', 'mp')
- grad_query: float32 [4096, 4096], P('dp', 'mp')
- grad_key: float32 [896, 4096], P('dp', 'mp')
- grad_value: float32 [896, 4096], P('dp', 'mp')
- grad_wout: float32 [4096, 4096], P('mp', 'dp')
The draws below stay inside these ranges and needn't reach their ends.
Inputs may be any that keep to these rules, and one draw needn't show every extreme that they name: `nb_owner`: among the 8 stretches of one index of dp no shard is named more than 3 times, a bound that some block reaches; the 2 neighbours of a stretch lie on different shards. `nb_len`: the first neighbour of every stretch has all 128 tokens.
All inputs are finite; a program needn't handle non-finite values.
Results may differ from the reference program's by a relative error of at most 0.014.
The reference program's roundings to bfloat16 on the way (of `normed`, `queries`, `blocks`, `prob`, `attended`, `grad_attn` and `grad_scores`) count: a program that leaves them out, or rounds other values in their place, can miss the bound.
Values may be sent and summed in bfloat16 or wider, within the bound.
A program may use at most 128 MiB of HBM per device.

```python
import math
import jax
import jax.numpy as jnp
import numpy as np
from jax import lax

D = 4096
HEADS = 32
HD = 128
ENC = 896
CL = 64
KN = 2
NL = 128
CAP = 3
DB_DEV = 24
STRETCH_DEV = 8
TOKENS = 4096
STRETCHES = 64
DBCHUNKS = 192
N_DP = 8
N_MP = 4


def draw_cache(key, part):
    base = jnp.clip(jax.random.normal(key, (DBCHUNKS, NL, ENC), jnp.float32), -6.0, 6.0)
    return base.astype(jnp.bfloat16)


def draw_nb_len(key, part):
    first_len = jnp.full((STRETCHES, 1), NL, jnp.int32)
    others = jax.random.randint(jax.random.fold_in(key, 3), (STRETCHES, KN - 1), NL // 4, NL + 1).astype(jnp.int32)
    return jnp.concatenate([first_len, others], axis=1)


def place_ends(array, rng, low, high):
    extent = array.shape
    index_at = [jax.random.randint(jax.random.fold_in(rng, axis), (), 0, extent[axis]) for axis in range(len(extent))]
    array = array.at[tuple(index_at)].set(low)
    longest = extent.index(max(extent))
    index_at[longest] = (index_at[longest] + 1) % extent[longest]
    return array.at[tuple(index_at)].set(high)


def with_spikes(result, key, source, target, shards_of, factor):
    def block_of(axis_at):
        return (jnp.arange(result.shape[axis_at]) // (result.shape[axis_at] // shards_of)).reshape((-1,) + (1,) * (result.ndim - 1 - axis_at))

    near = jax.random.permutation(key, shards_of)[block_of(target)]
    second = (block_of(target) + shards_of // 2) % shards_of
    return jnp.where((block_of(source) == near) | (block_of(source) == second), factor * result, result)


def shard_levels(stream_key, shape, split, low, high):
    loudness = 1.0
    for axis_at, parts in split:
        steps = jax.random.uniform(jax.random.fold_in(jax.random.fold_in(stream_key, 6), axis_at), (parts,), jnp.float32, low / len(split), high / len(split))
        loudness = loudness * jnp.repeat(jnp.exp(steps), shape[axis_at] // parts).reshape((-1,) + (1,) * (len(shape) - 1 - axis_at))
    return loudness


def shared_out(rng, own, number, rows, amount, top, most, skew):
    ranking = jax.random.permutation(rng, amount)
    heavy_load, ordinary = portions_of(amount, rows * top, most, skew, True), portions_of(amount, rows * top, most, skew, False)
    places = jnp.arange(amount)

    def named(tallies, rotation):
        used = int((tallies > 0).sum())
        fixed = max(1, used // 4)
        shifted = fixed + (places - fixed + rotation * (used - fixed)) % max(1, amount - fixed)
        return jnp.zeros((amount,), jnp.int32).at[ranking[jnp.where(places < fixed, places, shifted)]].set(jnp.asarray(tallies, jnp.int32))

    tallies = jnp.where(number % 4 == 0, named(heavy_load, number // 4), named(ordinary, number - number // 4 - 1))
    mixed = jax.random.permutation(jax.random.fold_in(own, 3), amount)
    donor, sink = mixed[0:amount // 2 * 2:2], mixed[1:amount // 2 * 2:2]
    room = jnp.minimum(tallies[donor] - 1, most - tallies[sink]) // 2
    room = jnp.where((donor == ranking[0]) | (sink == ranking[0]) | (tallies[sink] == 0), 0, jnp.maximum(room, 0))
    shifted = jax.random.randint(jax.random.fold_in(own, 4), (amount // 2,), 0, 1 << 20) % (room + 1)
    tallies = tallies.at[donor].add(-shifted).at[sink].add(shifted)
    labels = jnp.searchsorted(jnp.cumsum(tallies), jnp.arange(rows * top), side="right").astype(jnp.int32)
    listing = labels.reshape(top, rows).T
    listing = listing[jax.random.permutation(jax.random.fold_in(own, 1), rows)]
    rotation = jax.random.randint(jax.random.fold_in(own, 2), (rows, 1), 0, top)
    return jnp.take_along_axis(listing, (jnp.arange(top)[None, :] + rotation) % top, axis=1)


def portions_of(count, total, limit, lean, full):
    portions = [(1 << 20) // math.isqrt(rank ** lean) + 1 for rank in range(1, count + 1)]
    largest = limit if full else min(limit, max(-(-total // count), total * portions[0] // sum(portions)))
    least = 1 if total - largest >= count - 1 else 0
    counts, surplus = [largest] + [least] * (count - 1), total - largest - least * (count - 1)
    while surplus > 0:
        movable = [i for i in range(1, count) if counts[i] < largest] or [i for i in range(1, count) if counts[i] < limit]
        mass, budget = sum([portions[i] for i in movable]), surplus
        for i in movable:
            more = min(limit - counts[i], max(1, budget * portions[i] // mass), surplus)
            counts[i] = counts[i] + more
            surplus = surplus - more
    return np.array(counts)


def gaussian(rng, extent, spread, reach, pieces=(), kind=jnp.bfloat16):
    values = spread * jax.random.normal(rng, extent, jnp.float32)
    if pieces:
        values = values * shard_levels(rng, extent, pieces, -0.22, 0.18)
    return jnp.clip(values, -reach, reach).astype(kind)


def heavy_noise(rng, extent, spread, reach, cuts, heavy, held_as=jnp.bfloat16):
    result = spread * jax.random.normal(rng, extent, jnp.float32)
    if cuts:
        result = result * shard_levels(rng, extent, cuts, -0.22, 0.18)
    return jnp.clip(with_spikes(result, jax.random.fold_in(rng, 3), *heavy), -reach, reach).astype(held_as)


def setup_inputs(seed: int = 0) -> dict:
    arg_keys = jax.random.split(jax.random.key(seed), 11)
    tokens = heavy_noise(arg_keys[0], (TOKENS, D), 1.0, 6.0, ((0, 8),), (0, 1, 8, 2.0))
    cache = draw_cache(jax.random.fold_in(arg_keys[10], 71), 0)
    nb_row = place_ends(jax.random.randint(arg_keys[2], (STRETCHES, KN), 0, DB_DEV), jax.random.fold_in(arg_keys[2], 1), 0, DB_DEV - 1).astype(jnp.int32)
    nb_owner_keys = jax.random.split(jax.random.fold_in(arg_keys[3], 1), STRETCHES // STRETCH_DEV)
    nb_owner_turns = jax.random.permutation(jax.random.fold_in(arg_keys[3], 3), STRETCHES // STRETCH_DEV)
    nb_owner = jax.vmap(lambda own, number: shared_out(jax.random.fold_in(arg_keys[3], 2), own, number, STRETCH_DEV, N_DP, KN, CAP, 2))(nb_owner_keys, nb_owner_turns).reshape((STRETCHES, KN))
    nb_len = draw_nb_len(jax.random.fold_in(arg_keys[10], 71), 0)
    w_query = gaussian(arg_keys[5], (D, D), D ** -0.5, 0.09375, ((0, 8), (1, 4)))
    w_key = gaussian(arg_keys[6], (ENC, D), ENC ** -0.5, 0.1875, ((0, 8), (1, 4)))
    w_value = gaussian(arg_keys[7], (ENC, D), ENC ** -0.5, 0.1875, ((0, 8), (1, 4)))
    w_out = gaussian(arg_keys[8], (D, D), D ** -0.5, 0.09375, ((0, 4), (1, 8)))
    grad_out = heavy_noise(arg_keys[9], (TOKENS, D), 1.0, 6.0, ((0, 8),), (0, 1, 8, 2.0))
    return {"tokens": tokens, "cache": cache, "nb_row": nb_row, "nb_owner": nb_owner, "nb_len": nb_len, "w_query": w_query, "w_key": w_key, "w_value": w_value, "w_out": w_out, "grad_out": grad_out}


def group_heads(left_side, right_side, groups):
    span = left_side.shape[1] // groups
    summed = jnp.zeros((left_side.shape[0], right_side.shape[1]), jnp.float32)
    for group_index in range(groups):
        term = jnp.dot(left_side[:, group_index * span:(group_index + 1) * span], right_side[group_index * span:(group_index + 1) * span, :], preferred_element_type=jnp.float32).astype(jnp.bfloat16)
        term = lax.optimization_barrier(term)
        summed = summed + term.astype(jnp.float32)
    return summed

def group_rows(left_side, right_side, groups):
    span = left_side.shape[0] // groups
    summed = jnp.zeros((left_side.shape[1], right_side.shape[1]), jnp.float32)
    for group_index in range(groups):
        term = jnp.dot(left_side[group_index * span:(group_index + 1) * span].T, right_side[group_index * span:(group_index + 1) * span], preferred_element_type=jnp.float32).astype(jnp.bfloat16)
        term = lax.optimization_barrier(term)
        summed = summed + term.astype(jnp.float32)
    return summed

def one_stretch(stretch_item):
    query_block, key_block, value_block, key_valid, grad_block = stretch_item
    score_scale = HD ** (-0.5)
    query_wide = query_block.astype(jnp.float32)
    key_wide = key_block.astype(jnp.float32)
    value_wide = value_block.astype(jnp.float32)
    grad_wide = grad_block.astype(jnp.float32)
    scores = jnp.einsum('qhd,khd->hqk', query_wide, key_wide) * score_scale
    scores = jnp.where(key_valid[None, None, :], scores, -1e+30)
    row_top = lax.optimization_barrier(jnp.max(scores, axis=2, keepdims=True))
    weights_exp = jnp.exp(scores - row_top)
    prob_wide = weights_exp / lax.optimization_barrier(jnp.sum(weights_exp, axis=2, keepdims=True))
    prob = lax.optimization_barrier(prob_wide.astype(jnp.bfloat16)).astype(jnp.float32)
    attended = jnp.einsum('hqk,khd->qhd', prob, value_wide).astype(jnp.bfloat16)
    grad_prob = jnp.einsum('qhd,khd->hqk', grad_wide, value_wide)
    grad_values = jnp.einsum('hqk,qhd->khd', prob, grad_wide).astype(jnp.bfloat16)
    delta_rows = lax.optimization_barrier(jnp.sum(prob_wide * grad_prob, axis=2, keepdims=True))
    grad_scores = (prob_wide * (grad_prob - delta_rows) * score_scale).astype(jnp.bfloat16)
    grad_scores = lax.optimization_barrier(grad_scores).astype(jnp.float32)
    grad_queries = jnp.einsum('hqk,khd->qhd', grad_scores, key_wide).astype(jnp.bfloat16)
    grad_keys = jnp.einsum('hqk,qhd->khd', grad_scores, query_wide).astype(jnp.bfloat16)
    return (attended, grad_queries, grad_keys, grad_values)

def reference(tokens, cache, nb_row, nb_owner, nb_len, w_query, w_key, w_value, w_out, grad_out):
    wide_tokens = tokens.astype(jnp.float32)
    inv_rms = lax.rsqrt(lax.optimization_barrier(jnp.mean(wide_tokens * wide_tokens, axis=1, keepdims=True)) + 1e-06)
    normed_wide = wide_tokens * inv_rms
    normed = normed_wide.astype(jnp.bfloat16)
    queries = jnp.dot(normed, w_query, preferred_element_type=jnp.float32).astype(jnp.bfloat16)
    picked = (nb_owner * DB_DEV + nb_row).reshape(-1).astype(jnp.int32)
    blocks = jnp.take(cache, picked, axis=0)
    flat_blocks = blocks.reshape(STRETCHES * KN * NL, ENC)
    keys = jnp.dot(flat_blocks, w_key, preferred_element_type=jnp.float32).astype(jnp.bfloat16)
    values = jnp.dot(flat_blocks, w_value, preferred_element_type=jnp.float32).astype(jnp.bfloat16)
    grad_attn = jnp.dot(grad_out, w_out.T, preferred_element_type=jnp.float32).astype(jnp.bfloat16)
    positions = jnp.arange(NL, dtype=jnp.int32)
    key_valid = (positions[None, None, :] < nb_len[:, :, None]).reshape(STRETCHES, KN * NL)
    attended, grad_queries, grad_keys, grad_values = lax.map(one_stretch, (queries.reshape(STRETCHES, CL, HEADS, HD), keys.reshape(STRETCHES, KN * NL, HEADS, HD), values.reshape(STRETCHES, KN * NL, HEADS, HD), key_valid, grad_attn.reshape(STRETCHES, CL, HEADS, HD)))
    attended = attended.reshape(TOKENS, D)
    grad_queries = grad_queries.reshape(TOKENS, D)
    grad_keys = grad_keys.reshape(STRETCHES * KN * NL, D)
    grad_values = grad_values.reshape(STRETCHES * KN * NL, D)
    mixed = (wide_tokens + group_heads(attended, w_out, N_MP)).astype(jnp.bfloat16)
    grad_query = group_rows(normed, grad_queries, N_DP)
    grad_wout = group_rows(attended, grad_out, N_DP)
    grad_key = group_rows(flat_blocks, grad_keys, N_DP)
    grad_value = group_rows(flat_blocks, grad_values, N_DP)
    grad_normed = group_heads(grad_queries, w_query.T, N_MP)
    stat_rows = lax.optimization_barrier(jnp.mean(grad_normed * normed_wide, axis=1, keepdims=True))
    grad_tokens = (grad_out.astype(jnp.float32) + inv_rms * (grad_normed - normed_wide * stat_rows)).astype(jnp.bfloat16)
    return (mixed, grad_tokens, grad_query, grad_key, grad_value, grad_wout)
```

```python
import functools
import jax
import jax.numpy as jnp
from jax import lax
from jax.experimental import pallas as pl
from jax.experimental.pallas import tpu as pltpu
from jax.sharding import PartitionSpec as P

HD = 128
CL = 64
KN = 2
CAP = 3
MESH = pl.DeviceIdType.MESH
ANY = pl.BlockSpec(memory_space=pl.ANY)
SUB = 16


def places():
    me = lax.axis_index("dp")
    core, x, y = me % 2, (me // 2) % 2, me // 4
    sib = me + 1 - 2 * core
    dx, dy = 2 - 4 * x, 4 - 8 * y
    return me, sib, dx, dy


def greet(peers):
    barrier = pltpu.get_barrier_semaphore()
    for peer in peers:
        pl.semaphore_signal(barrier, inc=1, device_id={"dp": peer}, device_id_type=MESH)
    pl.semaphore_wait(barrier, len(peers))


def halves(rows):
    first = -(-(rows // 2) // SUB) * SUB
    return ((0, first), (first, rows - first))


def share_of(ref, axis, shape, index, start=0, size=None):
    rows, cols = shape
    size = rows if size is None else size
    if axis == 0:
        return ref.at[pl.ds(pl.multiple_of(index * rows + start, SUB), size), :]
    return ref.at[pl.ds(start, size), pl.ds(pl.multiple_of(index * cols, cols), cols)]


def gather_kernel(axes, shapes, *refs):
    count = len(axes)
    shards, fulls = refs[:count], refs[count : 2 * count]
    send, recv, local = refs[2 * count :]
    me, sib, dx, dy = places()
    greet((sib, me + dx, me + dy))
    started = []

    def place(a, owner, half):
        start, size = halves(shapes[a][0])[half]
        return share_of(fulls[a], axes[a], shapes[a], owner, start, size)

    def remote(a, source, owner, half, peer, slot):
        return pltpu.make_async_remote_copy(
            src_ref=source, dst_ref=place(a, owner, half), send_sem=send.at[a, slot],
            recv_sem=recv.at[a, slot], device_id={"dp": peer}, device_id_type=MESH)

    def push(a, source, owner, half, peer, slot):
        copy = remote(a, source, owner, half, peer, slot)
        copy.start()
        started.append(copy)

    def arrive(a, owner, half, slot):
        remote(a, place(a, owner, half), owner, half, sib, slot).wait_recv()

    own = []
    for a in range(count):
        parts = [shards[a].at[pl.ds(s, n), :] for s, n in halves(shapes[a][0])]
        push(a, parts[0], me, 0, me + dx, 0)
        push(a, parts[1], me, 1, me + dy, 3)
        push(a, parts[1], me, 1, me + dx, 1)
        push(a, parts[0], me, 0, me + dy, 2)
        for half in range(2):
            push(a, parts[half], me, half, sib, 4 + half)
            copy = pltpu.make_async_copy(parts[half], place(a, me, half), local.at[a, half])
            copy.start()
            own.append(copy)
    for a in range(count):
        near_x, near_y = me + dx, me + dy
        arrive(a, near_x, 0, 0)
        push(a, place(a, near_x, 0), near_x, 0, me + dy, 6)
        arrive(a, near_y, 1, 3)
        push(a, place(a, near_y, 1), near_y, 1, me + dx, 7)
        push(a, place(a, near_x, 0), near_x, 0, sib, 8)
        push(a, place(a, near_y, 1), near_y, 1, sib, 11)
        arrive(a, near_x, 1, 1)
        push(a, place(a, near_x, 1), near_x, 1, sib, 9)
        arrive(a, near_y, 0, 2)
        push(a, place(a, near_y, 0), near_y, 0, sib, 10)
    for a in range(count):
        far = me + dx + dy
        for half in range(2):
            arrive(a, far, half, 6 + half)
            push(a, place(a, far, half), far, half, sib, 12 + half)
    for a in range(count):
        for half in range(2):
            arrive(a, sib, half, 4 + half)
            arrive(a, sib + dx, half, 8 + half)
            arrive(a, sib + dy, half, 10 + half)
            arrive(a, sib + dx + dy, half, 12 + half)
    for copy in own:
        copy.wait()
    for copy in started:
        copy.wait_send()


def gather_all(shards, axes):
    dp_count = lax.axis_size("dp")
    if dp_count != 8:
        return [lax.all_gather(s, "dp", axis=a, tiled=True) for s, a in zip(shards, axes)]
    shapes = [s.shape for s in shards]
    outs = [jax.ShapeDtypeStruct((r * dp_count, c) if a == 0 else (r, c * dp_count), s.dtype)
            for s, a, (r, c) in zip(shards, axes, shapes)]
    count = len(shards)
    return pl.pallas_call(
        functools.partial(gather_kernel, axes, shapes),
        out_shape=outs,
        in_specs=[ANY] * count,
        out_specs=[ANY] * count,
        scratch_shapes=[pltpu.SemaphoreType.DMA((count, 14)), pltpu.SemaphoreType.DMA((count, 14)),
                        pltpu.SemaphoreType.DMA((count, 2))],
        compiler_params=pltpu.CompilerParams(collective_id=0, has_side_effects=True),
        name="gather_weights",
    )(*shards)


def scatter_kernel(axes, shapes, *refs):
    count = len(axes)
    parts, outs = refs[:count], refs[count : 2 * count]
    bufs = refs[2 * count : 6 * count]
    send, recv, local = refs[6 * count :]
    mine, cross = bufs[:count], bufs[count : 2 * count]
    via_x, via_y = bufs[2 * count : 3 * count], bufs[3 * count :]
    me, sib, dx, dy = places()
    moves = (0, dx, dy, dx + dy)
    near_x, near_y = me + dx, me + dy
    greet((sib, near_x, near_y))
    started, loads, crossings = [], {}, {}

    def push(a, source, target, peer, slot):
        copy = pltpu.make_async_remote_copy(
            src_ref=source, dst_ref=target, send_sem=send.at[a, slot],
            recv_sem=recv.at[a, slot], device_id={"dp": peer}, device_id_type=MESH)
        copy.start()
        started.append(copy)
        return copy

    def add(a, target, other, start, size):
        def step(i, _):
            rows = pl.ds(pl.multiple_of(start + i * SUB, SUB), SUB)
            target[rows, :] = (target[rows, :].astype(jnp.float32)
                               + other[rows, :].astype(jnp.float32)).astype(target.dtype)
            return 0
        lax.fori_loop(0, size // SUB, step, 0)

    for a in range(count):
        for r in (3, 1, 2, 0):
            crossings[a, r] = push(a, share_of(parts[a], axes[a], shapes[a], sib + moves[r]),
                                   cross[a].at[r], sib, r)
            load = pltpu.make_async_copy(share_of(parts[a], axes[a], shapes[a], me + moves[r]),
                                         mine[a].at[r], local.at[a, r])
            load.start()
            loads[a, r] = load
    hops = {}
    for a in range(count):
        rows = shapes[a][0]
        (a0, an), (b0, bn) = halves(rows)
        top, low = pl.ds(a0, an), pl.ds(b0, bn)
        for r in (3, 1, 2, 0):
            loads[a, r].wait()
            crossings[a, r].wait_recv()
            add(a, mine[a].at[r], cross[a].at[r], 0, rows)
            if r in (3, 1):
                k = r // 2
                hops[a, "x", k] = push(a, mine[a].at[r, top], via_x[a].at[k, top], near_x, 4 + k)
            if r in (3, 2):
                k = r - 2
                hops[a, "y", k] = push(a, mine[a].at[r, low], via_y[a].at[k, low], near_y, 6 + k)
    for a in range(count):
        (a0, an), (b0, bn) = halves(shapes[a][0])
        top, low = pl.ds(a0, an), pl.ds(b0, bn)
        hops[a, "x", 1].wait_recv()
        add(a, mine[a].at[2], via_x[a].at[1], a0, an)
        hops[a, "y", 2] = push(a, mine[a].at[2, top], via_y[a].at[0, top], near_y, 8)
        hops[a, "y", 1].wait_recv()
        add(a, mine[a].at[1], via_y[a].at[1], b0, bn)
        hops[a, "x", 2] = push(a, mine[a].at[1, low], via_x[a].at[0, low], near_x, 9)
    for a in range(count):
        for k in (0, 2):
            hops[a, "x", k].wait_recv()
            hops[a, "y", k].wait_recv()

        def finish(i, _, a=a):
            rows = pl.ds(pl.multiple_of(i * SUB, SUB), SUB)
            outs[a][rows, :] = (mine[a][0, rows, :].astype(jnp.float32)
                                + via_x[a][0, rows, :].astype(jnp.float32)
                                + via_y[a][0, rows, :].astype(jnp.float32))
            return 0
        lax.fori_loop(0, shapes[a][0] // SUB, finish, 0)
    for copy in started:
        copy.wait_send()


def scatter_all(parts, axes):
    dp_count = lax.axis_size("dp")
    if dp_count != 8:
        return [lax.psum_scatter(p, "dp", scatter_dimension=a, tiled=True).astype(jnp.float32)
                for p, a in zip(parts, axes)]
    shapes = [(p.shape[0] // dp_count, p.shape[1]) if a == 0 else (p.shape[0], p.shape[1] // dp_count)
              for p, a in zip(parts, axes)]
    count = len(parts)
    four = [pltpu.VMEM((4,) + s, jnp.bfloat16) for s in shapes]
    two = [pltpu.VMEM((2,) + s, jnp.bfloat16) for s in shapes]
    return pl.pallas_call(
        functools.partial(scatter_kernel, axes, shapes),
        out_shape=[jax.ShapeDtypeStruct(s, jnp.float32) for s in shapes],
        in_specs=[ANY] * count,
        out_specs=[pl.BlockSpec(memory_space=pltpu.VMEM)] * count,
        scratch_shapes=four + four + two + two
        + [pltpu.SemaphoreType.DMA((count, 10)), pltpu.SemaphoreType.DMA((count, 10)),
           pltpu.SemaphoreType.DMA((count, 4))],
        compiler_params=pltpu.CompilerParams(
            collective_id=1, has_side_effects=True, vmem_limit_bytes=56 * 2**20),
        name="scatter_gradients",
    )(*parts)


def pick_kernel(count, span, ids, source, out, sems):
    copies = []
    for i in range(count):
        row = source.at[ids[i], pl.ds(pl.multiple_of(ids[count] * span, SUB), span)]
        copy = pltpu.make_async_copy(row, out.at[i], sems.at[i])
        copy.start()
        copies.append(copy)
    for copy in copies:
        copy.wait()


def pick(source, ids, part, span):
    count = ids.shape[0]
    table = jnp.concatenate([ids, jnp.reshape(part, (1,))]).astype(jnp.int32)
    return pl.pallas_call(
        functools.partial(pick_kernel, count, span),
        out_shape=jax.ShapeDtypeStruct((count, span, source.shape[2]), source.dtype),
        in_specs=[pl.BlockSpec(memory_space=pltpu.SMEM), ANY],
        out_specs=ANY,
        scratch_shapes=[pltpu.SemaphoreType.DMA((count,))],
        name="pick_blocks",
    )(table, source)


def attend_kernel(heads, block_len, lens, q_ref, k_ref, v_ref, g_ref, att_ref, gq_ref, gk_ref, gv_ref):
    stretch = pl.program_id(0)
    scale = HD ** (-0.5)
    rows, span = q_ref.shape[0], k_ref.shape[0]
    at = lax.broadcasted_iota(jnp.int32, (rows, span), 1)
    valid = at < lens[stretch, 0]
    for j in range(1, KN):
        valid |= (at >= j * block_len) & (at < j * block_len + lens[stretch, j])

    def dot(left, right, sides):
        return lax.dot_general(left, right, (sides, ((), ())), preferred_element_type=jnp.float32)

    for h in range(heads):
        cols = slice(h * HD, (h + 1) * HD)
        q, k, v, g = q_ref[:, cols], k_ref[:, cols], v_ref[:, cols], g_ref[:, cols]
        scores = jnp.where(valid, dot(q, k, ((1,), (1,))) * scale, -1e30)
        expd = jnp.exp(scores - jnp.max(scores, axis=1, keepdims=True))
        wide = expd / jnp.sum(expd, axis=1, keepdims=True)
        prob = wide.astype(jnp.bfloat16)
        att_ref[:, cols] = dot(prob, v, ((1,), (0,))).astype(jnp.bfloat16)
        grad_prob = dot(g, v, ((1,), (1,)))
        gv_ref[:, cols] = dot(prob, g, ((0,), (0,))).astype(jnp.bfloat16)
        delta = jnp.sum(wide * grad_prob, axis=1, keepdims=True)
        grad_scores = (wide * (grad_prob - delta) * scale).astype(jnp.bfloat16)
        gq_ref[:, cols] = dot(grad_scores, k, ((1,), (0,))).astype(jnp.bfloat16)
        gk_ref[:, cols] = dot(grad_scores, q, ((0,), (0,))).astype(jnp.bfloat16)


def attend(nb_len, queries, keys, values, grads, block_len):
    stretches, width = nb_len.shape[0], queries.shape[1]
    small = pl.BlockSpec((CL, width), lambda c, lens: (c, 0))
    large = pl.BlockSpec((KN * block_len, width), lambda c, lens: (c, 0))
    like = lambda a: jax.ShapeDtypeStruct(a.shape, jnp.bfloat16)
    return pl.pallas_call(
        functools.partial(attend_kernel, width // HD, block_len),
        out_shape=[like(queries), like(queries), like(keys), like(values)],
        grid_spec=pltpu.PrefetchScalarGridSpec(
            num_scalar_prefetch=1, grid=(stretches,),
            in_specs=[small, large, large, small],
            out_specs=[small, small, large, large]),
        compiler_params=pltpu.CompilerParams(vmem_limit_bytes=32 * 2**20),
        name="attend",
    )(nb_len, queries, keys, values, grads)


def on_device(tokens, cache, nb_row, nb_owner, nb_len, w_query, w_key, w_value, w_out, grad_out):
    dp_count = lax.axis_size("dp")
    mp_count = lax.axis_size("mp")
    mp_place = lax.axis_index("mp")
    tok_rows, width = tokens.shape
    head_span = w_query.shape[1]
    heads_here = head_span // HD
    stretch_count = nb_row.shape[0]
    request_count = stretch_count * KN
    cache_rows, block_len, enc_width = cache.shape
    width_share = width // mp_count
    wide_tokens = tokens.astype(jnp.float32)
    inv_rms = lax.rsqrt(jnp.mean(wide_tokens * wide_tokens, axis=1, keepdims=True) + 1e-06)
    normed_wide = wide_tokens * inv_rms
    normed = normed_wide.astype(jnp.bfloat16)
    owners = nb_owner.reshape(-1)
    wanted = nb_row.reshape(-1)
    req_order = jnp.arange(request_count)
    earlier = (owners[:, None] == owners[None, :]) & (req_order[None, :] < req_order[:, None])
    rank_seen = jnp.sum(earlier.astype(jnp.int32), axis=1)
    slot_of = owners * CAP + rank_seen
    slot_hits = (slot_of[:, None] == jnp.arange(dp_count * CAP)[None, :]).astype(jnp.int32)
    asked_ids = (jnp.sum(slot_hits * (wanted[:, None] + 1), axis=0) - 1).reshape(dp_count, CAP)
    picked_rows = jnp.clip(
        lax.all_to_all(asked_ids, "dp", split_axis=0, concat_axis=0, tiled=True), 0, cache_rows - 1
    )
    span = block_len // mp_count
    picked = pick(cache, picked_rows.reshape(-1), mp_place, span)
    picked = picked.reshape(dp_count, CAP, span, enc_width)
    arrived = lax.all_to_all(picked, "dp", split_axis=0, concat_axis=0, tiled=True)
    arrived = arrived.reshape(dp_count * CAP, span, enc_width)
    chosen = pick(arrived, slot_of, jnp.int32(0), span)
    blocks = lax.all_gather(chosen, "mp", axis=1, tiled=True)
    flat_blocks = blocks.reshape(request_count * block_len, enc_width)
    query_full, output_full, key_full, value_full = gather_all(
        (w_query, w_out, w_key, w_value), (0, 1, 0, 0)
    )
    queries = jnp.dot(normed, query_full, preferred_element_type=jnp.float32).astype(jnp.bfloat16)
    grad_attn = jnp.einsum(
        "td,sd->ts", grad_out, output_full, preferred_element_type=jnp.float32
    ).astype(jnp.bfloat16)
    keys = jnp.dot(flat_blocks, key_full, preferred_element_type=jnp.float32).astype(jnp.bfloat16)
    values = jnp.dot(flat_blocks, value_full, preferred_element_type=jnp.float32).astype(jnp.bfloat16)
    attended, grad_queries, grad_keys, grad_values = attend(
        nb_len, queries, keys, values, grad_attn, block_len
    )
    partial_out = jnp.dot(attended, output_full, preferred_element_type=jnp.float32)
    summed_out = lax.psum_scatter(
        partial_out.astype(jnp.bfloat16), "mp", scatter_dimension=1, tiled=True
    ).astype(jnp.float32)
    token_cols = lax.dynamic_slice_in_dim(tokens, mp_place * width_share, width_share, 1).astype(
        jnp.float32
    )
    mixed = (token_cols + summed_out).astype(jnp.bfloat16)
    grad_wout_part = jnp.einsum("ts,td->sd", attended, grad_out, preferred_element_type=jnp.float32)
    grad_wq_part = jnp.einsum("td,ts->ds", normed, grad_queries, preferred_element_type=jnp.float32)
    grad_wk_part = jnp.einsum(
        "re,rs->es", flat_blocks, grad_keys, preferred_element_type=jnp.float32
    )
    grad_wv_part = jnp.einsum(
        "re,rs->es", flat_blocks, grad_values, preferred_element_type=jnp.float32
    )
    grad_query, grad_wout, grad_key, grad_value = scatter_all(
        [p.astype(jnp.bfloat16) for p in (grad_wq_part, grad_wout_part, grad_wk_part, grad_wv_part)],
        (0, 1, 0, 0),
    )
    grad_normed_part = jnp.einsum(
        "ts,ds->td", grad_queries, query_full, preferred_element_type=jnp.float32
    )
    out_cols = lax.dynamic_slice_in_dim(grad_out, mp_place * width_share, width_share, 1).astype(
        jnp.float32
    )
    normed_cols = token_cols * inv_rms
    grad_normed = lax.psum_scatter(
        grad_normed_part.astype(jnp.bfloat16), "mp", scatter_dimension=1, tiled=True
    ).astype(jnp.float32)
    stat_part = jnp.sum(grad_normed * normed_cols, axis=1, keepdims=True)
    stat_rows = lax.psum(stat_part, "mp") / width
    grad_here = inv_rms * (grad_normed - normed_cols * stat_rows)
    grad_tokens = (out_cols + grad_here).astype(jnp.bfloat16)
    return (mixed, grad_tokens, grad_query, grad_key, grad_value, grad_wout)


def solution(mesh):
    return jax.shard_map(
        on_device,
        mesh=mesh,
        in_specs=(
            P("dp", None),
            P("dp", None, None),
            P("dp", None),
            P("dp", None),
            P("dp", None),
            P("dp", "mp"),
            P("dp", "mp"),
            P("dp", "mp"),
            P("mp", "dp"),
            P("dp", None),
        ),
        out_specs=(
            P("dp", "mp"),
            P("dp", "mp"),
            P("dp", "mp"),
            P("dp", "mp"),
            P("dp", "mp"),
            P("mp", "dp"),
        ),
        check_vma=False,
    )
```

```python
import functools
import jax
import jax.numpy as jnp
from jax import lax
from jax.experimental import pallas as pl
from jax.experimental.pallas import tpu as pltpu
from jax.sharding import PartitionSpec as P

HD = 128
CL = 64
KN = 2
CAP = 3
MESH = pl.DeviceIdType.MESH
ANY = pl.BlockSpec(memory_space=pl.ANY)
SUB = 16


def places():
    me = lax.axis_index("dp")
    core, x, y = me % 2, (me // 2) % 2, me // 4
    sib = me + 1 - 2 * core
    dx, dy = 2 - 4 * x, 4 - 8 * y
    return me, sib, dx, dy


def greet(peers):
    barrier = pltpu.get_barrier_semaphore()
    for peer in peers:
        pl.semaphore_signal(barrier, inc=1, device_id={"dp": peer}, device_id_type=MESH)
    pl.semaphore_wait(barrier, len(peers))


def halves(rows):
    first = -(-(rows // 2) // SUB) * SUB
    return ((0, first), (first, rows - first))


def share_of(ref, axis, shape, index, start=0, size=None):
    rows, cols = shape
    size = rows if size is None else size
    if axis == 0:
        return ref.at[pl.ds(pl.multiple_of(index * rows + start, SUB), size), :]
    return ref.at[pl.ds(start, size), pl.ds(pl.multiple_of(index * cols, cols), cols)]


def gather_kernel(axes, shapes, *refs):
    count = len(axes)
    shards, fulls = refs[:count], refs[count : 2 * count]
    send, recv, local = refs[2 * count :]
    me, sib, dx, dy = places()
    greet((sib, me + dx, me + dy))
    started = []

    def place(a, owner, half):
        start, size = halves(shapes[a][0])[half]
        return share_of(fulls[a], axes[a], shapes[a], owner, start, size)

    def remote(a, source, owner, half, peer, slot):
        return pltpu.make_async_remote_copy(
            src_ref=source, dst_ref=place(a, owner, half), send_sem=send.at[a, slot],
            recv_sem=recv.at[a, slot], device_id={"dp": peer}, device_id_type=MESH)

    def push(a, source, owner, half, peer, slot):
        copy = remote(a, source, owner, half, peer, slot)
        copy.start()
        started.append(copy)

    def arrive(a, owner, half, slot):
        remote(a, place(a, owner, half), owner, half, sib, slot).wait_recv()

    own = []
    for a in range(count):
        parts = [shards[a].at[pl.ds(s, n), :] for s, n in halves(shapes[a][0])]
        push(a, parts[0], me, 0, me + dx, 0)
        push(a, parts[1], me, 1, me + dy, 3)
        push(a, parts[1], me, 1, me + dx, 1)
        push(a, parts[0], me, 0, me + dy, 2)
        for half in range(2):
            push(a, parts[half], me, half, sib, 4 + half)
            copy = pltpu.make_async_copy(parts[half], place(a, me, half), local.at[a, half])
            copy.start()
            own.append(copy)
    for a in range(count):
        near_x, near_y = me + dx, me + dy
        arrive(a, near_x, 0, 0)
        push(a, place(a, near_x, 0), near_x, 0, me + dy, 6)
        arrive(a, near_y, 1, 3)
        push(a, place(a, near_y, 1), near_y, 1, me + dx, 7)
        push(a, place(a, near_x, 0), near_x, 0, sib, 8)
        push(a, place(a, near_y, 1), near_y, 1, sib, 11)
        arrive(a, near_x, 1, 1)
        push(a, place(a, near_x, 1), near_x, 1, sib, 9)
        arrive(a, near_y, 0, 2)
        push(a, place(a, near_y, 0), near_y, 0, sib, 10)
    for a in range(count):
        far = me + dx + dy
        for half in range(2):
            arrive(a, far, half, 6 + half)
            push(a, place(a, far, half), far, half, sib, 12 + half)
    for a in range(count):
        for half in range(2):
            arrive(a, sib, half, 4 + half)
            arrive(a, sib + dx, half, 8 + half)
            arrive(a, sib + dy, half, 10 + half)
            arrive(a, sib + dx + dy, half, 12 + half)
    for copy in own:
        copy.wait()
    for copy in started:
        copy.wait_send()


def gather_all(shards, axes, number):
    dp_count = lax.axis_size("dp")
    if dp_count != 8:
        return [lax.all_gather(s, "dp", axis=a, tiled=True) for s, a in zip(shards, axes)]
    shapes = [s.shape for s in shards]
    outs = [jax.ShapeDtypeStruct((r * dp_count, c) if a == 0 else (r, c * dp_count), s.dtype)
            for s, a, (r, c) in zip(shards, axes, shapes)]
    count = len(shards)
    return pl.pallas_call(
        functools.partial(gather_kernel, axes, shapes),
        out_shape=outs,
        in_specs=[ANY] * count,
        out_specs=[ANY] * count,
        scratch_shapes=[pltpu.SemaphoreType.DMA((count, 14)), pltpu.SemaphoreType.DMA((count, 14)),
                        pltpu.SemaphoreType.DMA((count, 2))],
        compiler_params=pltpu.CompilerParams(collective_id=number, has_side_effects=True),
        cost_estimate=pl.CostEstimate(
            flops=0, transcendentals=0,
            bytes_accessed=sum(40 * dp_count * s.size for s in shards)),
        name="gather_weights",
    )(*shards)


def scatter_kernel(axes, shapes, *refs):
    count = len(axes)
    parts, outs = refs[:count], refs[count : 2 * count]
    bufs = refs[2 * count : 6 * count]
    send, recv, local = refs[6 * count :]
    mine, cross = bufs[:count], bufs[count : 2 * count]
    via_x, via_y = bufs[2 * count : 3 * count], bufs[3 * count :]
    me, sib, dx, dy = places()
    moves = (0, dx, dy, dx + dy)
    near_x, near_y = me + dx, me + dy
    greet((sib, near_x, near_y))
    started, loads, crossings = [], {}, {}

    def push(a, source, target, peer, slot):
        copy = pltpu.make_async_remote_copy(
            src_ref=source, dst_ref=target, send_sem=send.at[a, slot],
            recv_sem=recv.at[a, slot], device_id={"dp": peer}, device_id_type=MESH)
        copy.start()
        started.append(copy)
        return copy

    def add(a, target, other, start, size):
        def step(i, _):
            rows = pl.ds(pl.multiple_of(start + i * SUB, SUB), SUB)
            target[rows, :] = (target[rows, :].astype(jnp.float32)
                               + other[rows, :].astype(jnp.float32)).astype(target.dtype)
            return 0
        lax.fori_loop(0, size // SUB, step, 0)

    for a in range(count):
        for r in (3, 1, 2, 0):
            crossings[a, r] = push(a, share_of(parts[a], axes[a], shapes[a], sib + moves[r]),
                                   cross[a].at[r], sib, r)
            load = pltpu.make_async_copy(share_of(parts[a], axes[a], shapes[a], me + moves[r]),
                                         mine[a].at[r], local.at[a, r])
            load.start()
            loads[a, r] = load
    hops = {}
    for a in range(count):
        rows = shapes[a][0]
        (a0, an), (b0, bn) = halves(rows)
        top, low = pl.ds(a0, an), pl.ds(b0, bn)
        for r in (3, 1, 2, 0):
            loads[a, r].wait()
            crossings[a, r].wait_recv()
            add(a, mine[a].at[r], cross[a].at[r], 0, rows)
            if r in (3, 1):
                k = r // 2
                hops[a, "x", k] = push(a, mine[a].at[r, top], via_x[a].at[k, top], near_x, 4 + k)
            if r in (3, 2):
                k = r - 2
                hops[a, "y", k] = push(a, mine[a].at[r, low], via_y[a].at[k, low], near_y, 6 + k)
    for a in range(count):
        (a0, an), (b0, bn) = halves(shapes[a][0])
        top, low = pl.ds(a0, an), pl.ds(b0, bn)
        hops[a, "x", 1].wait_recv()
        add(a, mine[a].at[2], via_x[a].at[1], a0, an)
        hops[a, "y", 2] = push(a, mine[a].at[2, top], via_y[a].at[0, top], near_y, 8)
        hops[a, "y", 1].wait_recv()
        add(a, mine[a].at[1], via_y[a].at[1], b0, bn)
        hops[a, "x", 2] = push(a, mine[a].at[1, low], via_x[a].at[0, low], near_x, 9)
    for a in range(count):
        for k in (0, 2):
            hops[a, "x", k].wait_recv()
            hops[a, "y", k].wait_recv()

        def finish(i, _, a=a):
            rows = pl.ds(pl.multiple_of(i * SUB, SUB), SUB)
            outs[a][rows, :] = (mine[a][0, rows, :].astype(jnp.float32)
                                + via_x[a][0, rows, :].astype(jnp.float32)
                                + via_y[a][0, rows, :].astype(jnp.float32))
            return 0
        lax.fori_loop(0, shapes[a][0] // SUB, finish, 0)
    for copy in started:
        copy.wait_send()


def scatter_all(parts, axes):
    dp_count = lax.axis_size("dp")
    if dp_count != 8:
        return [lax.psum_scatter(p, "dp", scatter_dimension=a, tiled=True).astype(jnp.float32)
                for p, a in zip(parts, axes)]
    shapes = [(p.shape[0] // dp_count, p.shape[1]) if a == 0 else (p.shape[0], p.shape[1] // dp_count)
              for p, a in zip(parts, axes)]
    count = len(parts)
    four = [pltpu.VMEM((4,) + s, jnp.bfloat16) for s in shapes]
    two = [pltpu.VMEM((2,) + s, jnp.bfloat16) for s in shapes]
    return pl.pallas_call(
        functools.partial(scatter_kernel, axes, shapes),
        out_shape=[jax.ShapeDtypeStruct(s, jnp.float32) for s in shapes],
        in_specs=[ANY] * count,
        out_specs=[pl.BlockSpec(memory_space=pltpu.VMEM)] * count,
        scratch_shapes=four + four + two + two
        + [pltpu.SemaphoreType.DMA((count, 10)), pltpu.SemaphoreType.DMA((count, 10)),
           pltpu.SemaphoreType.DMA((count, 4))],
        compiler_params=pltpu.CompilerParams(
            collective_id=2, has_side_effects=True, vmem_limit_bytes=56 * 2**20),
        name="scatter_gradients",
    )(*parts)


def pick_kernel(count, span, ids, source, out, sems):
    copies = []
    for i in range(count):
        row = source.at[ids[i], pl.ds(pl.multiple_of(ids[count] * span, SUB), span)]
        copy = pltpu.make_async_copy(row, out.at[i], sems.at[i])
        copy.start()
        copies.append(copy)
    for copy in copies:
        copy.wait()


def pick(source, ids, part, span):
    count = ids.shape[0]
    table = jnp.concatenate([ids, jnp.reshape(part, (1,))]).astype(jnp.int32)
    return pl.pallas_call(
        functools.partial(pick_kernel, count, span),
        out_shape=jax.ShapeDtypeStruct((count, span, source.shape[2]), source.dtype),
        in_specs=[pl.BlockSpec(memory_space=pltpu.SMEM), ANY],
        out_specs=pl.BlockSpec(memory_space=pltpu.VMEM),
        scratch_shapes=[pltpu.SemaphoreType.DMA((count,))],
        name="pick_blocks",
    )(table, source)


def attend_kernel(heads, block_len, lens, q_ref, k_ref, v_ref, g_ref, att_ref, gq_ref, gk_ref, gv_ref):
    stretch = pl.program_id(0)
    scale = HD ** (-0.5)
    rows, span = q_ref.shape[0], k_ref.shape[0]
    at = lax.broadcasted_iota(jnp.int32, (rows, span), 1)
    valid = at < lens[stretch, 0]
    for j in range(1, KN):
        valid |= (at >= j * block_len) & (at < j * block_len + lens[stretch, j])

    def dot(left, right, sides):
        return lax.dot_general(left, right, (sides, ((), ())), preferred_element_type=jnp.float32)

    for h in range(heads):
        cols = slice(h * HD, (h + 1) * HD)
        q, k, v, g = q_ref[:, cols], k_ref[:, cols], v_ref[:, cols], g_ref[:, cols]
        scores = jnp.where(valid, dot(q, k, ((1,), (1,))) * scale, -1e30)
        expd = jnp.exp(scores - jnp.max(scores, axis=1, keepdims=True))
        wide = expd / jnp.sum(expd, axis=1, keepdims=True)
        prob = wide.astype(jnp.bfloat16)
        att_ref[:, cols] = dot(prob, v, ((1,), (0,))).astype(jnp.bfloat16)
        grad_prob = dot(g, v, ((1,), (1,)))
        gv_ref[:, cols] = dot(prob, g, ((0,), (0,))).astype(jnp.bfloat16)
        delta = jnp.sum(wide * grad_prob, axis=1, keepdims=True)
        grad_scores = (wide * (grad_prob - delta) * scale).astype(jnp.bfloat16)
        gq_ref[:, cols] = dot(grad_scores, k, ((1,), (0,))).astype(jnp.bfloat16)
        gk_ref[:, cols] = dot(grad_scores, q, ((0,), (0,))).astype(jnp.bfloat16)


def attend(nb_len, queries, keys, values, grads, block_len):
    stretches, width = nb_len.shape[0], queries.shape[1]
    small = pl.BlockSpec((CL, width), lambda c, lens: (c, 0))
    large = pl.BlockSpec((KN * block_len, width), lambda c, lens: (c, 0))
    like = lambda a: jax.ShapeDtypeStruct(a.shape, jnp.bfloat16)
    return pl.pallas_call(
        functools.partial(attend_kernel, width // HD, block_len),
        out_shape=[like(queries), like(queries), like(keys), like(values)],
        grid_spec=pltpu.PrefetchScalarGridSpec(
            num_scalar_prefetch=1, grid=(stretches,),
            in_specs=[small, large, large, small],
            out_specs=[small, small, large, large]),
        compiler_params=pltpu.CompilerParams(vmem_limit_bytes=32 * 2**20),
        name="attend",
    )(nb_len, queries, keys, values, grads)


def on_device(tokens, cache, nb_row, nb_owner, nb_len, w_query, w_key, w_value, w_out, grad_out):
    dp_count = lax.axis_size("dp")
    mp_count = lax.axis_size("mp")
    mp_place = lax.axis_index("mp")
    tok_rows, width = tokens.shape
    head_span = w_query.shape[1]
    heads_here = head_span // HD
    stretch_count = nb_row.shape[0]
    request_count = stretch_count * KN
    cache_rows, block_len, enc_width = cache.shape
    width_share = width // mp_count
    wide_tokens = tokens.astype(jnp.float32)
    inv_rms = lax.rsqrt(jnp.mean(wide_tokens * wide_tokens, axis=1, keepdims=True) + 1e-06)
    normed_wide = wide_tokens * inv_rms
    normed = normed_wide.astype(jnp.bfloat16)
    owners = nb_owner.reshape(-1)
    wanted = nb_row.reshape(-1)
    req_order = jnp.arange(request_count)
    earlier = (owners[:, None] == owners[None, :]) & (req_order[None, :] < req_order[:, None])
    rank_seen = jnp.sum(earlier.astype(jnp.int32), axis=1)
    slot_of = owners * CAP + rank_seen
    slot_hits = (slot_of[:, None] == jnp.arange(dp_count * CAP)[None, :]).astype(jnp.int32)
    asked_ids = (jnp.sum(slot_hits * (wanted[:, None] + 1), axis=0) - 1).reshape(dp_count, CAP)
    picked_rows = jnp.clip(
        lax.all_to_all(asked_ids, "dp", split_axis=0, concat_axis=0, tiled=True), 0, cache_rows - 1
    )
    span = block_len // mp_count
    picked = pick(cache, picked_rows.reshape(-1), mp_place, span)
    picked = picked.reshape(dp_count, CAP, span, enc_width)
    picked, w_out = lax.optimization_barrier((picked, w_out))
    (output_full,) = gather_all((w_out,), (1,), 0)
    arrived = lax.all_to_all(picked, "dp", split_axis=0, concat_axis=0, tiled=True)
    arrived, output_full = lax.optimization_barrier((arrived, output_full))
    arrived = arrived.reshape(dp_count * CAP, span, enc_width)
    chosen = pick(arrived, slot_of, jnp.int32(0), span)
    chosen, w_query = lax.optimization_barrier((chosen, w_query))
    blocks = lax.all_gather(chosen, "mp", axis=1, tiled=True)
    flat_blocks = blocks.reshape(request_count * block_len, enc_width)
    query_full, key_full, value_full = gather_all((w_query, w_key, w_value), (0, 0, 0), 1)
    queries = jnp.dot(normed, query_full, preferred_element_type=jnp.float32).astype(jnp.bfloat16)
    grad_attn = jnp.einsum(
        "td,sd->ts", grad_out, output_full, preferred_element_type=jnp.float32
    ).astype(jnp.bfloat16)
    keys = jnp.dot(flat_blocks, key_full, preferred_element_type=jnp.float32).astype(jnp.bfloat16)
    values = jnp.dot(flat_blocks, value_full, preferred_element_type=jnp.float32).astype(jnp.bfloat16)
    attended, grad_queries, grad_keys, grad_values = attend(
        nb_len, queries, keys, values, grad_attn, block_len
    )
    partial_out = jnp.dot(attended, output_full, preferred_element_type=jnp.float32)
    summed_out = lax.psum_scatter(
        partial_out.astype(jnp.bfloat16), "mp", scatter_dimension=1, tiled=True
    ).astype(jnp.float32)
    token_cols = lax.dynamic_slice_in_dim(tokens, mp_place * width_share, width_share, 1).astype(
        jnp.float32
    )
    mixed = (token_cols + summed_out).astype(jnp.bfloat16)
    grad_wout_part = jnp.einsum("ts,td->sd", attended, grad_out, preferred_element_type=jnp.float32)
    grad_wq_part = jnp.einsum("td,ts->ds", normed, grad_queries, preferred_element_type=jnp.float32)
    grad_wk_part = jnp.einsum(
        "re,rs->es", flat_blocks, grad_keys, preferred_element_type=jnp.float32
    )
    grad_wv_part = jnp.einsum(
        "re,rs->es", flat_blocks, grad_values, preferred_element_type=jnp.float32
    )
    grad_query, grad_wout, grad_key, grad_value = scatter_all(
        [p.astype(jnp.bfloat16) for p in (grad_wq_part, grad_wout_part, grad_wk_part, grad_wv_part)],
        (0, 1, 0, 0),
    )
    grad_normed_part = jnp.einsum(
        "ts,ds->td", grad_queries, query_full, preferred_element_type=jnp.float32
    )
    out_cols = lax.dynamic_slice_in_dim(grad_out, mp_place * width_share, width_share, 1).astype(
        jnp.float32
    )
    normed_cols = token_cols * inv_rms
    grad_normed = lax.psum_scatter(
        grad_normed_part.astype(jnp.bfloat16), "mp", scatter_dimension=1, tiled=True
    ).astype(jnp.float32)
    stat_part = jnp.sum(grad_normed * normed_cols, axis=1, keepdims=True)
    stat_rows = lax.psum(stat_part, "mp") / width
    grad_here = inv_rms * (grad_normed - normed_cols * stat_rows)
    grad_tokens = (out_cols + grad_here).astype(jnp.bfloat16)
    return (mixed, grad_tokens, grad_query, grad_key, grad_value, grad_wout)


def solution(mesh):
    return jax.shard_map(
        on_device,
        mesh=mesh,
        in_specs=(
            P("dp", None),
            P("dp", None, None),
            P("dp", None),
            P("dp", None),
            P("dp", None),
            P("dp", "mp"),
            P("dp", "mp"),
            P("dp", "mp"),
            P("mp", "dp"),
            P("dp", None),
        ),
        out_specs=(
            P("dp", "mp"),
            P("dp", "mp"),
            P("dp", "mp"),
            P("dp", "mp"),
            P("dp", "mp"),
            P("mp", "dp"),
        ),
        check_vma=False,
    )
```
